512 devices in a mesh: dp: 4 (over x), expert: 16 (over z), tensor: 8 (over y, core).
Axes of the slice: x: 4, y: 4, z: 16, core: 2. Of those that a mesh axis runs over, the one named last changes fastest.
Arguments:
- tokens: bfloat16 [1024, 4096], P(('dp', 'expert'), 'tensor'), may hold values from -6 to 6
- expert_ids: int32 [1024, 3], P(('dp', 'expert')), may hold values from 0 to 15, all different within a row; in each aligned block of 16 rows (0 to 15, 16 to 31, ...) at most 4 rows name the same one
- route_weights: float32 [1024, 3], P(('dp', 'expert')), may hold values from 0.1 to 1
- gate_weight: bfloat16 [16, 5120, 4096], P('expert', ('dp', 'tensor')), may hold values from -0.09375 to 0.09375
- up_weight: bfloat16 [16, 5120, 4096], P('expert', ('dp', 'tensor')), may hold values from -0.09375 to 0.09375
- down_weight: bfloat16 [16, 5120, 4096], P('expert', ('dp', 'tensor')), may hold values from -0.15625 to 0.15625
Outputs:
- mixed: bfloat16 [1024, 4096], P(('dp', 'expert'), 'tensor')
The draws below stay inside these ranges and needn't reach their ends.
Inputs may be any that keep to these rules, and one draw needn't show every extreme that they name: `expert_ids`: A row's 3 ids differ. In the rows of one device (aligned blocks of 16 rows) no expert is picked by more than 4 rows, and in every block some expert is picked by exactly 4 rows.
All inputs are finite; a program needn't handle non-finite values.
Results may differ from the reference program's by a relative error of at most 0.02.
Values may be sent and summed in bfloat16 or wider, within the bound.
A program may use at most 64 MiB of HBM per device.

```python
import math
import jax
import jax.numpy as jnp
import numpy as np
from jax import lax

D = 4096
FF = 5120
TOP = 3
TOK_DEV = 16
EXPERTS = 16
CAP = 4
ROWS = 1024
N_DP = 4
N_EXPERT = 16
N_TENSOR = 8


def with_spikes(drawn, key, source, target, blocks, factor):
    def block_of(position):
        return (jnp.arange(drawn.shape[position]) // (drawn.shape[position] // blocks)).reshape((-1,) + (1,) * (drawn.ndim - 1 - position))

    first = jax.random.permutation(key, blocks)[block_of(target)]
    second = (block_of(target) + blocks // 2) % blocks
    return jnp.where((block_of(source) == first) | (block_of(source) == second), factor * drawn, drawn)


def steps_of(stream_key, extent, cuts, smallest, high):
    level, own = 1.0, jax.random.fold_in(stream_key, 6)
    for position, shards_of in cuts:
        steps = jnp.exp(jax.random.uniform(jax.random.fold_in(own, position), (shards_of,), jnp.float32, smallest / len(cuts), high / len(cuts)))
        level = level * jnp.repeat(steps, extent[position] // shards_of).reshape([-1 if axis == position else 1 for axis in range(len(extent))])
    return level


def shared_out(rng, own, number, rows, amount, top, limit, skew):
    sequence = jax.random.permutation(rng, amount)
    packed, usual = shares(amount, rows * top, limit, skew, True), shares(amount, rows * top, limit, skew, False)
    places = jnp.arange(amount)

    def named(lengths, offset_by):
        used = int((lengths > 0).sum())
        fixed = max(1, used // 4)
        passed = fixed + (places - fixed + offset_by * (used - fixed)) % max(1, amount - fixed)
        return jnp.zeros((amount,), jnp.int32).at[sequence[jnp.where(places < fixed, places, passed)]].set(jnp.asarray(lengths, jnp.int32))

    lengths = jnp.where(number % 4 == 0, named(packed, number // 4), named(usual, number - number // 4 - 1))
    mixed = jax.random.permutation(jax.random.fold_in(own, 3), amount)
    source_of, taker = mixed[0:amount // 2 * 2:2], mixed[1:amount // 2 * 2:2]
    room = jnp.minimum(lengths[source_of] - 1, limit - lengths[taker]) // 2
    room = jnp.where((source_of == sequence[0]) | (taker == sequence[0]) | (lengths[taker] == 0), 0, jnp.maximum(room, 0))
    passed = jax.random.randint(jax.random.fold_in(own, 4), (amount // 2,), 0, 1 << 20) % (room + 1)
    lengths = lengths.at[source_of].add(-passed).at[taker].add(passed)
    labels = jnp.searchsorted(jnp.cumsum(lengths), jnp.arange(rows * top), side="right").astype(jnp.int32)
    listing = labels.reshape(top, rows).T
    listing = listing[jax.random.permutation(jax.random.fold_in(own, 1), rows)]
    offset_by = jax.random.randint(jax.random.fold_in(own, 2), (rows, 1), 0, top)
    return jnp.take_along_axis(listing, (jnp.arange(top)[None, :] + offset_by) % top, axis=1)


def shares(amount, total, most, lean, full):
    portions = [(1 << 20) // math.isqrt(rank ** lean) + 1 for rank in range(1, amount + 1)]
    largest = most if full else min(most, max(-(-total // amount), total * portions[0] // sum(portions)))
    least = 1 if total - largest >= amount - 1 else 0
    holding, rest = [largest] + [least] * (amount - 1), total - largest - least * (amount - 1)
    while rest > 0:
        free = [i for i in range(1, amount) if holding[i] < largest] or [i for i in range(1, amount) if holding[i] < most]
        whole, remaining = sum([portions[i] for i in free]), rest
        for i in free:
            addition = min(most - holding[i], max(1, remaining * portions[i] // whole), rest)
            holding[i] = holding[i] + addition
            rest = rest - addition
    return np.array(holding)


def noise(own_key, shape, spread, reach, shards=(), kind=jnp.bfloat16):
    values = spread * jax.random.normal(own_key, shape, jnp.float32)
    if shards:
        values = values * steps_of(own_key, shape, shards, -0.22, 0.18)
    return jnp.clip(values, -reach, reach).astype(kind)


def noise_with(rng, shape, scale, most, shards, heavy, held_as=jnp.bfloat16):
    values = scale * jax.random.normal(rng, shape, jnp.float32)
    if shards:
        values = values * steps_of(rng, shape, shards, -0.22, 0.18)
    return jnp.clip(with_spikes(values, jax.random.fold_in(rng, 3), *heavy), -most, most).astype(held_as)


def setup_inputs(seed: int = 0) -> dict:
    keys = jax.random.split(jax.random.key(seed), 7)
    tokens = noise(keys[0], (ROWS, D), 1.0, 6.0, ((0, 64), (1, 8)))
    expert_ids_keys = jax.random.split(jax.random.fold_in(keys[1], 1), ROWS // TOK_DEV)
    expert_ids_turns = jax.random.permutation(jax.random.fold_in(keys[1], 3), ROWS // TOK_DEV)
    expert_ids = jax.vmap(lambda own, number: shared_out(jax.random.fold_in(keys[1], 2), own, number, TOK_DEV, EXPERTS, TOP, CAP, 2))(expert_ids_keys, expert_ids_turns).reshape((ROWS, TOP))
    route_weights = jnp.clip(0.1 + 0.9 * jax.random.uniform(keys[2], (ROWS, TOP), jnp.float32) ** steps_of(keys[2], (ROWS, TOP), ((0, 64),), -0.2, 0.2), 0.1, 1.0)
    gate_weight = noise(keys[3], (EXPERTS, FF, D), D ** -0.5, 0.09375, ((0, 16), (1, 32)))
    up_weight = noise(keys[4], (EXPERTS, FF, D), D ** -0.5, 0.09375, ((0, 16), (1, 32)))
    down_weight = noise_with(keys[5], (EXPERTS, FF, D), FF ** -0.5, 0.15625, ((0, 16), (1, 32)), (1, 2, 32, 2.75))
    return {"tokens": tokens, "expert_ids": expert_ids, "route_weights": route_weights, "gate_weight": gate_weight, "up_weight": up_weight, "down_weight": down_weight}


def project_rows(chosen, weight_rows):
    return lax.dot_general(chosen, weight_rows, (((1,), (1,)), ((), ())), preferred_element_type=jnp.float32)


def reference(tokens, expert_ids, route_weights, gate_weight, up_weight, down_weight):
    load = CAP * N_DP * N_EXPERT
    groups = N_DP * N_TENSOR
    width = FF // groups
    width_model = tokens.shape[1]

    def one_expert(index):
        hit = expert_ids == index
        weight = jnp.sum(jnp.where(hit, route_weights, jnp.zeros_like(route_weights)), axis=1)
        picked = jnp.any(hit, axis=1).astype(jnp.int32)
        order = jnp.argsort(1 - picked, stable=True)[:load].astype(jnp.int32)
        chosen = tokens[order]
        gate = project_rows(chosen, gate_weight[index])
        up_part = project_rows(chosen, up_weight[index])
        hidden = (jax.nn.silu(gate) * up_part).astype(jnp.bfloat16)
        blocks = hidden.reshape(load, groups, width).astype(jnp.float32)
        downs = down_weight[index].reshape(groups, width, width_model).astype(jnp.float32)
        parts = jnp.einsum("ngf,gfd->gnd", blocks, downs)
        rounded = lax.optimization_barrier(parts.astype(jnp.bfloat16))
        output = jnp.sum(rounded.astype(jnp.float32), axis=0).astype(jnp.bfloat16)
        contrib = weight[order][:, None] * output.astype(jnp.float32)
        return order, contrib

    orders, contribs = lax.map(one_expert, jnp.arange(EXPERTS, dtype=jnp.int32))
    total = jnp.zeros(tokens.shape, jnp.float32)
    total = total.at[orders.reshape(-1)].add(contribs.reshape(-1, width_model))
    return total.astype(jnp.bfloat16)
```

```python
import jax
import jax.numpy as jnp
from jax import lax
from jax.experimental import pallas as pl
from jax.experimental.pallas import tpu as pltpu
from jax.sharding import PartitionSpec as P

MESH = pl.DeviceIdType.MESH
BF16 = jnp.bfloat16
F32 = jnp.float32
NX, NZ, NY = 4, 16, 4
CHUNKS = ((0, 1, -1, 2, -2, 3, -3, 4), (-4, 5, -5, 6, -6, 7, -7, 8))
NCH = len(CHUNKS)
SLOTS = 4
LANES = 128
FAR_FIRST = (2, 1, 3)


def iota(shape, dim):
    return lax.broadcasted_iota(jnp.int32, shape, dim)


def unfold_matrix(count, transposed):
    size = 16 * count
    row, col = iota((size, size), 0), iota((size, size), 1)
    if transposed:
        row, col = col, row
    wanted = (row % (SLOTS * count)) // SLOTS * 16 + row // (SLOTS * count) * SLOTS + row % SLOTS
    return jnp.where(wanted == col, 1.0, 0.0).astype(BF16)


def kernel(tok_hbm, ids_hbm, rw_hbm, wg_hbm, wu_hbm, wd_hbm, out_ref,
           tok, ids, rw, wg, wu, wd, ob, zr, xg, sc, rc, own, s1, r1x, r1y, s2x, s2y, r2x, r2y, fo, rb,
           load_sem, send_sem, z_sem, p1_sem, p2_sem, core_sem, rcore_sem, q1x_sem, q1y_sem, q2x_sem, q2y_sem, back_sem):
    x, z, t = lax.axis_index("dp"), lax.axis_index("expert"), lax.axis_index("tensor")
    y, c = t // 2, t % 2
    per = SLOTS * len(CHUNKS[0])

    def dev(dx=0, dz=0, dy=0, twin=False):
        other = 1 - c if twin else c
        return ((x + dx + NX) % NX, (z + dz + NZ) % NZ, (y + dy) % NY * 2 + other)

    barrier = pltpu.get_barrier_semaphore()
    partners = [dict(dz=d) for d in (8, 7, 9, 6, 10, 5, 11, 4, 12, 3, 13, 2, 14, 1, 15)]
    partners += [dict(dx=d) for d in FAR_FIRST] + [dict(dy=d) for d in FAR_FIRST] + [dict(twin=True)]
    for partner in partners:
        pl.semaphore_signal(barrier, inc=1, device_id=dev(**partner), device_id_type=MESH)

    loads = [
        pltpu.make_async_copy(ids_hbm, ids, load_sem.at[0]),
        pltpu.make_async_copy(rw_hbm, rw, load_sem.at[1]),
        pltpu.make_async_copy(tok_hbm, tok, load_sem.at[2]),
        pltpu.make_async_copy(wg_hbm.at[0], wg, load_sem.at[3]),
        pltpu.make_async_copy(wu_hbm.at[0], wu, load_sem.at[4]),
    ]
    for i in range(8):
        loads.append(pltpu.make_async_copy(wd_hbm.at[0, :, pl.ds(i * 512, 512)], wd.at[i], load_sem.at[5 + i]))
    for load in loads:
        load.start()

    sent = []

    def send(src, dst, sem, device):
        copy = pltpu.make_async_remote_copy(
            src_ref=src, dst_ref=dst, send_sem=send_sem.at[len(sent)], recv_sem=sem,
            device_id=device, device_id_type=MESH)
        copy.start()
        sent.append(copy)

    def arrived(ref, sem):
        pltpu.make_async_copy(ref, ref, sem).wait()

    for load in loads[:3]:
        load.wait()
    shape = (16, 256)
    q = iota(shape, 1)
    hits = [ids[:, k:k + 1] == q // 16 for k in range(3)]
    hit = jnp.where(hits[0] | hits[1] | hits[2], 1.0, 0.0)
    below = jnp.where(iota((16, 16), 0) > iota((16, 16), 1), 1.0, 0.0)
    place = jnp.dot(below.astype(BF16), hit.astype(BF16), preferred_element_type=F32)
    here = place == (q % SLOTS).astype(F32)
    picked = jnp.where(here, hit, 0.0)
    weight = jnp.zeros(shape, F32)
    for k in range(3):
        weight = weight + jnp.where(hits[k] & here, rw[:, k:k + 1], 0.0)
    piece = q // SLOTS % 4
    pick_rows = jnp.concatenate([jnp.where(piece == j, picked, 0.0) for j in range(4)], axis=0).astype(BF16)
    weights = jnp.concatenate([jnp.where(piece == j, weight, 0.0) for j in range(4)], axis=0)
    token_pieces = jnp.concatenate([tok[:, j * LANES:(j + 1) * LANES] for j in range(4)], axis=0)
    slot_rows = lax.dot_general(pick_rows, token_pieces, (((0,), (0,)), ((), ())), preferred_element_type=F32)
    ob[...] = slot_rows.astype(BF16).reshape(16, 16, LANES)
    zr[0] = ob[z]

    pl.semaphore_wait(barrier, len(partners))

    for k in reversed(range(NCH)):
        for i in reversed(range(len(CHUNKS[k]))):
            d = CHUNKS[k][i]
            if d != 0:
                send(ob.at[(z - d + NZ) % NZ], zr.at[k * len(CHUNKS[0]) + i], z_sem.at[k], dev(dz=-d))

    count = len(CHUNKS[0])
    unfold = unfold_matrix(count, False)
    fold = unfold_matrix(count, True)

    def gather_start(k):
        first = k * count
        own_place = 1 if k == 0 else 0
        arrived(zr.at[pl.ds(first + own_place, count - own_place)], z_sem.at[k])
        folded = zr[pl.ds(first, count)].reshape(count * 16, LANES)
        rows = jnp.dot(unfold, folded, preferred_element_type=F32).astype(BF16)
        for j in range(4):
            xg[k, c, y, j // 2, 0, :, (j % 2) * LANES:(j % 2 + 1) * LANES] = rows[j * per:(j + 1) * per]
        for i in FAR_FIRST:
            send(xg.at[k, c, y, 0, 0], xg.at[k, c, y, 0, 4 - i], p1_sem.at[k, 0, i - 1], dev(dx=i))
            send(xg.at[k, c, y, 1, 0], xg.at[k, c, y, 1, 0], p1_sem.at[k, 1, i - 1], dev(dy=i))
        forward(k, 0, 0)
        forward(k, 1, 0)

    def forward(k, h, i):
        if h == 0:
            place = xg.at[k, c, y, 0, (4 - i) % 4]
            if i:
                arrived(place, p1_sem.at[k, 0, i - 1])
            for j in FAR_FIRST:
                send(place, place, p2_sem.at[k, 0, j - 1], dev(dy=j))
        else:
            line = (y - i + 4) % 4
            place = xg.at[k, c, line, 1, 0]
            if i:
                arrived(place, p1_sem.at[k, 1, i - 1])
            for j in FAR_FIRST:
                send(place, xg.at[k, c, line, 1, 4 - j], p2_sem.at[k, 1, j - 1], dev(dx=j))

    def group(k, h, g, core):
        if h == 0:
            return xg.at[k, core, (y - g + 4) % 4, 0]
        return xg.at[k, core, pl.ds(0, 4), 1, (4 - g) % 4]

    def to_twin(k, h, g):
        place = group(k, h, g, c)
        if g:
            arrived(place, p2_sem.at[k, h, g - 1])
        send(place, place, core_sem.at[k, h, g], dev(twin=True))

    def gather_end(k):
        for h in range(2):
            for g in range(4):
                arrived(group(k, h, g, 1 - c), core_sem.at[k, h, g])

    def hidden_of(k):
        gate = up = jnp.zeros((4 * per, 160), F32)
        for core in range(2):
            for line in range(4):
                for h in range(2):
                    left = xg[k, core, line, h].reshape(4 * per, 256)
                    start = (line * 2 + core) * 512 + h * 256
                    dims = (((1,), (1,)), ((), ()))
                    gate = gate + lax.dot_general(left, wg[:, start:start + 256], dims, preferred_element_type=F32)
                    up = up + lax.dot_general(left, wu[:, start:start + 256], dims, preferred_element_type=F32)
        return (gate / (1.0 + jnp.exp(-gate)) * up).astype(BF16)

    def down(k, hidden, j, twin):
        out = jnp.dot(hidden, wd[(y + j) % 4 * 2 + (1 - c if twin else c)], preferred_element_type=F32)
        for h in range(2):
            part = out[:, h * 256:(h + 1) * 256].reshape(4, per, 256)
            if twin:
                sc[k, j, h] = part.astype(BF16)
            else:
                own[k, j, h] = part
        if twin:
            send(sc.at[k, j], rc.at[k, j], rcore_sem.at[k, j], dev(twin=True))

    def sum_cores(k, j):
        arrived(rc.at[k, j], rcore_sem.at[k, j])
        first = own[k, j, 0] + rc[k, j, 0].astype(F32)
        own[k, j, 0, 0] = first[0]
        s1[k, j, 0] = first.astype(BF16)
        for i in FAR_FIRST:
            send(s1.at[k, j, 0, i], r1x.at[k, i - 1, j], q1x_sem.at[k, i - 1], dev(dx=i))
        second = own[k, j, 1] + rc[k, j, 1].astype(F32)
        if j:
            s1[k, j, 1] = second.astype(BF16)
            send(s1.at[k, j, 1], r1y.at[k, j - 1], q1y_sem.at[k, j - 1], dev(dy=j))
        else:
            own[k, 0, 1] = second

    def sum_first(k):
        for i in range(3):
            arrived(r1y.at[k, i], q1y_sem.at[k, i])
        for i in FAR_FIRST + (0,):
            total = own[k, 0, 1, i]
            for n in range(3):
                total = total + r1y[k, n, i].astype(F32)
            if i:
                s2y[k, i - 1] = total.astype(BF16)
                send(s2y.at[k, i - 1], r2y.at[k, i - 1], q2y_sem.at[k, i - 1], dev(dx=i))
            else:
                own[k, 0, 1, 0] = total
        for i in range(3):
            arrived(r1x.at[k, i], q1x_sem.at[k, i])
        for j in FAR_FIRST + (0,):
            total = own[k, j, 0, 0]
            for n in range(3):
                total = total + r1x[k, n, j].astype(F32)
            if j:
                s2x[k, j - 1] = total.astype(BF16)
                send(s2x.at[k, j - 1], r2x.at[k, j - 1], q2x_sem.at[k, j - 1], dev(dy=j))
            else:
                own[k, 0, 0, 0] = total

    def send_back(k):
        pieces = []
        for h, landed, sem in ((0, r2x, q2x_sem), (1, r2y, q2y_sem)):
            total = own[k, 0, h, 0]
            for n in range(3):
                arrived(landed.at[k, n], sem.at[k, n])
                total = total + landed[k, n].astype(F32)
            total = total.astype(BF16)
            pieces += [total[:, :LANES], total[:, LANES:]]
        rows = jnp.dot(fold, jnp.concatenate(pieces, axis=0), preferred_element_type=F32).astype(BF16)
        fo[pl.ds(k * count, count)] = rows.reshape(count, 16, LANES)
        for i in reversed(range(count)):
            d = CHUNKS[k][i]
            if d:
                send(fo.at[k * count + i], rb.at[z], back_sem.at[0], dev(dz=d))
            else:
                rb[z] = fo[k * count + i]

    schedule(gather_start, forward, to_twin, gather_end, hidden_of, down, sum_cores, sum_first, send_back, loads)

    arrived(rb.at[pl.ds(0, NZ - 1)], back_sem.at[0])
    high = weights.astype(BF16)
    rest = weights - high.astype(F32)
    middle = rest.astype(BF16)
    low = (rest - middle.astype(F32)).astype(BF16)
    stacked = jnp.concatenate([high, middle, low], axis=0)
    mixed = jnp.dot(stacked, rb[...].reshape(256, LANES), preferred_element_type=F32)
    mixed = mixed[:64] + mixed[64:128] + mixed[128:]
    for j in range(4):
        out_ref[:, j * LANES:(j + 1) * LANES] = mixed[j * 16:(j + 1) * 16].astype(BF16)
    for copy in sent:
        copy.wait_send()


def schedule(gather_start, forward, to_twin, gather_end, hidden_of, down, sum_cores, sum_first, send_back, loads):
    def hand_on(k):
        for i in (1, 3, 2):
            for h in range(2):
                forward(k, h, i)
        for h in range(2):
            to_twin(k, h, 0)

    def hand_over(k):
        for g in (1, 3, 2):
            for h in range(2):
                to_twin(k, h, g)

    def multiply(k):
        hidden = hidden_of(k)
        for twin in (True, False):
            for j in FAR_FIRST + (0,):
                down(k, hidden, j, twin)

    def spread(k):
        for j in FAR_FIRST + (0,):
            sum_cores(k, j)

    gather_start(0)
    hand_on(0)
    gather_start(1)
    hand_over(0)
    hand_on(1)
    for load in loads[3:]:
        load.wait()
    gather_end(0)
    multiply(0)
    hand_over(1)
    spread(0)
    gather_end(1)
    multiply(1)
    sum_first(0)
    spread(1)
    send_back(0)
    sum_first(1)
    send_back(1)


def on_device(*args):
    per = SLOTS * len(CHUNKS[0])
    dma = lambda *shape: pltpu.SemaphoreType.DMA(shape)
    vmem = pltpu.VMEM
    return pl.pallas_call(
        kernel,
        out_shape=jax.ShapeDtypeStruct((16, 512), BF16),
        in_specs=[pl.BlockSpec(memory_space=pl.ANY)] * 6,
        out_specs=pl.BlockSpec(memory_space=pltpu.VMEM),
        scratch_shapes=[
            vmem((16, 512), BF16), vmem((16, 3), jnp.int32), vmem((16, 3), F32),
            vmem((160, 4096), BF16), vmem((160, 4096), BF16), vmem((8, 160, 512), BF16),
            vmem((16, 16, LANES), BF16), vmem((16, 16, LANES), BF16),
            vmem((NCH, 2, 4, 2, 4, per, 256), BF16),
            vmem((NCH, 4, 2, 4, per, 256), BF16), vmem((NCH, 4, 2, 4, per, 256), BF16),
            vmem((NCH, 4, 2, 4, per, 256), F32),
            vmem((NCH, 4, 2, 4, per, 256), BF16),
            vmem((NCH, 3, 4, per, 256), BF16), vmem((NCH, 3, 4, per, 256), BF16),
            vmem((NCH, 3, per, 256), BF16), vmem((NCH, 3, per, 256), BF16),
            vmem((NCH, 3, per, 256), BF16), vmem((NCH, 3, per, 256), BF16),
            vmem((16, 16, LANES), BF16), vmem((16, 16, LANES), BF16),
            dma(13), dma(30 + NCH * 63), dma(NCH),
            dma(NCH, 2, 3), dma(NCH, 2, 3), dma(NCH, 2, 4), dma(NCH, 4),
            dma(NCH, 3), dma(NCH, 3), dma(NCH, 3), dma(NCH, 3), dma(1),
        ],
        compiler_params=pltpu.CompilerParams(
            collective_id=0, has_side_effects=True, vmem_limit_bytes=40 << 20),
        name="experts",
    )(*args)


def solution(mesh):
    placed = (
        P(("dp", "expert"), "tensor"),
        P(("dp", "expert"), None),
        P(("dp", "expert"), None),
        P("expert", ("dp", "tensor"), None),
        P("expert", ("dp", "tensor"), None),
        P("expert", ("dp", "tensor"), None),
    )
    return jax.shard_map(
        on_device,
        mesh=mesh,
        in_specs=placed,
        out_specs=P(("dp", "expert"), "tensor"),
        check_vma=False,
    )
```

```python
import jax
import jax.numpy as jnp
from jax import lax
from jax.experimental import pallas as pl
from jax.experimental.pallas import tpu as pltpu
from jax.sharding import PartitionSpec as P

MESH = pl.DeviceIdType.MESH
BF16 = jnp.bfloat16
F32 = jnp.float32
NZ = 16
SLOTS = 4
LANES = 128
PIECES = 4
HID = 160
COUNT = 4
ROWS = COUNT * SLOTS
FAR_FIRST = (2, 1, 3)
IN_ORDER = (0, 1, 3, 2)


def iota(shape, dim):
    return lax.broadcasted_iota(jnp.int32, shape, dim)


def source_of(core, k, i):
    return 4 * k + i - core * (4 + 8 * k)


def place_of(expert):
    source = (8 - expert) % NZ - 8
    if source >= 0:
        return 0, source // 4, source % 4
    return 1, int(source < -4), source % 4


def unfold_matrix(transposed):
    size = 16 * COUNT
    row, col = iota((size, size), 0), iota((size, size), 1)
    if transposed:
        row, col = col, row
    wanted = (row % ROWS) // SLOTS * 16 + row // ROWS * SLOTS + row % SLOTS
    return jnp.where(wanted == col, 1.0, 0.0).astype(BF16)


def kernel(tok_hbm, ids_hbm, rw_hbm, wg_hbm, wu_hbm, wd_hbm, out_ref,
           tok, ids, rw, wg, wu, wd, ob, mix, up_held, down_held, zr, xg, own0, own1, s1x, s1y, r1x, r1y, s2x, s2y, r2x, r2y, fo, rb,
           load_sem, twin_sem, twin_send, send_sem, self_send, z_sem, hold_sem, p1_sem, p2_sem, q1x_sem, q1y_sem, q2x_sem, q2y_sem,
           back_sem):
    x, z, t = lax.axis_index("dp"), lax.axis_index("expert"), lax.axis_index("tensor")
    y, c = t // 2, t % 2

    def dev(dx=0, dz=0, dy=0, core=c):
        return ((x + dx + 4) % 4, (z + dz + NZ) % NZ, (y + dy) % 4 * 2 + core)

    barrier = pltpu.get_barrier_semaphore()
    loads = [
        pltpu.make_async_copy(ids_hbm, ids, load_sem.at[0]),
        pltpu.make_async_copy(rw_hbm, rw, load_sem.at[1]),
        pltpu.make_async_copy(tok_hbm, tok, load_sem.at[2]),
        pltpu.make_async_copy(wg_hbm.at[0], wg.at[pl.ds(0, HID)], load_sem.at[3]),
        pltpu.make_async_copy(wu_hbm.at[0], wu.at[pl.ds(0, HID)], load_sem.at[4]),
    ]
    for i in range(8):
        loads.append(pltpu.make_async_copy(wd_hbm.at[0, :, pl.ds(i * 512, 512)], wd.at[i, pl.ds(0, HID)], load_sem.at[5 + i]))
    for load in loads[:3]:
        load.start()
    partners = [dict(dz=d, core=core) for d in (4, -4, 3, -3, 2, -2, 1, -1) for core in range(2)]
    partners += [dict(dx=d) for d in FAR_FIRST] + [dict(dy=d) for d in FAR_FIRST] + [dict(core=1 - c)]
    for partner in partners:
        pl.semaphore_signal(barrier, inc=1, device_id=dev(**partner), device_id_type=MESH)
    for load in loads[3:]:
        load.start()

    sent = []

    def send(src, dst, sem, device):
        copy = pltpu.make_async_remote_copy(
            src_ref=src, dst_ref=dst, send_sem=send_sem.at[len(sent)], recv_sem=sem,
            device_id=device, device_id_type=MESH)
        copy.start()
        sent.append(copy)

    def arrived(ref, sem):
        pltpu.make_async_copy(ref, ref, sem).wait()

    for load in loads[:3]:
        load.wait()
    shape = (256, 64)
    q, lane = iota(shape, 0), iota(shape, 1)
    steps_up = (ids[...] - z + NZ) % NZ
    ids_wide = jnp.concatenate([steps_up] * PIECES, axis=1)
    rw_wide = jnp.concatenate([rw[...]] * PIECES, axis=1)
    hits = [ids_wide[k:k + 1] == q // 16 for k in range(3)]
    hit = jnp.where(hits[0] | hits[1] | hits[2], 1.0, 0.0)
    source, row = iota((64, 64), 0), iota((64, 64), 1)
    below = jnp.where((source // 16 == row // 16) & (source < row), 1.0, 0.0)
    place = jnp.dot(hit.astype(BF16), below.astype(BF16), preferred_element_type=F32)
    here = (place == (q % SLOTS).astype(F32)) & (q // SLOTS % PIECES == lane // 16)
    picked = jnp.where(here, hit, 0.0).astype(BF16)
    weights = jnp.zeros(shape, F32)
    for k in range(3):
        weights = weights + jnp.where(hits[k] & here, rw_wide[k:k + 1], 0.0)
    token_pieces = jnp.concatenate([tok[:, j * LANES:(j + 1) * LANES] for j in range(PIECES)], axis=0)
    slot_rows = jnp.dot(picked, token_pieces, preferred_element_type=F32)
    ob[...] = slot_rows.astype(BF16).reshape(16, 16, LANES)
    unfold = unfold_matrix(False)
    fold = unfold_matrix(True)

    pl.semaphore_wait(barrier, len(partners))

    send(ob.at[pl.ds(5, 4)], up_held, hold_sem.at[0], dev(dz=4))
    send(ob.at[pl.ds(9, 3)], down_held, hold_sem.at[1], dev(dz=-4))
    for d in (4, -4, 3, -3, 2, -2, 1, -1):
        core, k, i = place_of(d)
        send(ob.at[d % NZ], zr.at[k, c, i], z_sem.at[k], dev(dz=d, core=core))
    to_self = pltpu.make_async_copy(ob.at[0], zr.at[0, 0, 0], z_sem.at[0])
    to_near = pltpu.make_async_remote_copy(
        src_ref=ob.at[0], dst_ref=zr.at[0, 1, 0], send_sem=self_send.at[0], recv_sem=z_sem.at[0],
        device_id=dev(core=0), device_id_type=MESH)
    pl.when(c == 0)(to_self.start)
    pl.when(c == 1)(to_near.start)

    to_twin = []

    def twin(src, dst):
        n = len(to_twin)
        copy = pltpu.make_async_remote_copy(
            src_ref=src, dst_ref=dst, send_sem=twin_send.at[n], recv_sem=twin_sem.at[n],
            device_id=dev(core=1 - c), device_id_type=MESH)
        copy.start()
        to_twin.append(copy)

    twin(wg_hbm.at[0], wg.at[pl.ds(HID, HID)])
    twin(wu_hbm.at[0], wu.at[pl.ds(HID, HID)])
    for i in range(8):
        twin(wd_hbm.at[0, :, pl.ds(i * 512, 512)], wd.at[i, pl.ds(HID, HID)])

    by_row = weights.T
    high = by_row.astype(BF16)
    rest = by_row - high.astype(F32)
    middle = rest.astype(BF16)
    mix[0:64] = high
    mix[64:128] = middle
    mix[128:192] = (rest - middle.astype(F32)).astype(BF16)

    arrived(up_held, hold_sem.at[0])
    for n in range(4):
        core, k, i = place_of(5 + n)
        send(up_held.at[n], zr.at[k, c, i], z_sem.at[k], dev(dz=1 + n, core=core))
    arrived(down_held, hold_sem.at[1])
    for n in range(3):
        core, k, i = place_of(9 + n)
        send(down_held.at[n], zr.at[k, c, i], z_sem.at[k], dev(dz=n - 3, core=core))

    def forward(k, h, i):
        if h == 0:
            place = xg.at[k, 0, y, (4 - i) % 4]
            if i:
                arrived(place, p1_sem.at[k, 0, i - 1])
            for j in FAR_FIRST:
                send(place, place, p2_sem.at[k, 0, j - 1], dev(dy=j))
        else:
            line = (y - i + 4) % 4
            place = xg.at[k, 1, line, 0]
            if i:
                arrived(place, p1_sem.at[k, 1, i - 1])
            for j in FAR_FIRST:
                send(place, xg.at[k, 1, line, 4 - j], p2_sem.at[k, 1, j - 1], dev(dx=j))

    def gather_start(k):
        arrived(zr.at[k], z_sem.at[k])
        for h in range(2):
            rows = jnp.dot(unfold, zr[k, h].reshape(COUNT * 16, LANES), preferred_element_type=F32).astype(BF16)
            for j in range(PIECES):
                xg[k, h, y, 0, :, j * LANES:(j + 1) * LANES] = rows[j * ROWS:(j + 1) * ROWS]
            for i in FAR_FIRST:
                if h == 0:
                    send(xg.at[k, 0, y, 0], xg.at[k, 0, y, 4 - i], p1_sem.at[k, 0, i - 1], dev(dx=i))
                else:
                    send(xg.at[k, 1, y, 0], xg.at[k, 1, y, 0], p1_sem.at[k, 1, i - 1], dev(dy=i))
        for h in range(2):
            forward(k, h, 0)

    def hand_on(k):
        for i in IN_ORDER[1:]:
            for h in range(2):
                forward(k, h, i)

    def gather_end(k):
        for j in IN_ORDER[1:]:
            arrived(xg.at[k, 0, (y - j + 4) % 4], p2_sem.at[k, 0, j - 1])
            arrived(xg.at[k, 1, pl.ds(0, 4), 4 - j], p2_sem.at[k, 1, j - 1])

    def hidden_of(k):
        gate = up = jnp.zeros((4 * ROWS, 2 * HID), F32)
        for h in range(2):
            for line in range(4):
                left = xg[k, h, line].reshape(4 * ROWS, 512)
                start = (line * 2 + h) * 512
                dims = (((1,), (1,)), ((), ()))
                gate = gate + lax.dot_general(left, wg[:, start:start + 512], dims, preferred_element_type=F32)
                up = up + lax.dot_general(left, wu[:, start:start + 512], dims, preferred_element_type=F32)
        return (gate / (1.0 + jnp.exp(-gate)) * up).astype(BF16)

    def spread(k, hidden):
        for j in FAR_FIRST + (0,):
            for h in range(2):
                out = jnp.dot(hidden, wd[(y + j) % 4 * 2 + h], preferred_element_type=F32).reshape(4, ROWS, 512)
                if h == 0:
                    own0[k, j] = out[0]
                    s1x[k, j] = out[1:].astype(BF16)
                    for i in FAR_FIRST:
                        send(s1x.at[k, j, i - 1], r1x.at[k, i - 1, j], q1x_sem.at[k, i - 1], dev(dx=i))
                elif j:
                    s1y[k, j - 1] = out.astype(BF16)
                    send(s1y.at[k, j - 1], r1y.at[k, j - 1], q1y_sem.at[k, j - 1], dev(dy=j))
                else:
                    own1[k] = out

    def sum_first(k):
        for n in range(3):
            arrived(r1y.at[k, n], q1y_sem.at[k, n])
        for i in FAR_FIRST + (0,):
            total = own1[k, i]
            for n in range(3):
                total = total + r1y[k, n, i].astype(F32)
            if i:
                s2y[k, i - 1] = total.astype(BF16)
                send(s2y.at[k, i - 1], r2y.at[k, i - 1], q2y_sem.at[k, i - 1], dev(dx=i))
            else:
                own1[k, 0] = total
        for n in range(3):
            arrived(r1x.at[k, n], q1x_sem.at[k, n])
        for j in FAR_FIRST + (0,):
            total = own0[k, j]
            for n in range(3):
                total = total + r1x[k, n, j].astype(F32)
            if j:
                s2x[k, j - 1] = total.astype(BF16)
                send(s2x.at[k, j - 1], r2x.at[k, j - 1], q2x_sem.at[k, j - 1], dev(dy=j))
            else:
                own0[k, 0] = total

    def send_back(k):
        for h, own, landed, sem in ((1, own1, r2y, q2y_sem), (0, own0, r2x, q2x_sem)):
            total = own[k, 0]
            for n in range(3):
                arrived(landed.at[k, n], sem.at[k, n])
                total = total + landed[k, n].astype(F32)
            total = total.astype(BF16)
            pieces = [total[:, j * LANES:(j + 1) * LANES] for j in range(PIECES)]
            rows = jnp.dot(fold, jnp.concatenate(pieces, axis=0), preferred_element_type=F32).astype(BF16)
            fo[k, h] = rows.reshape(COUNT, 16, LANES)
            for i in reversed(range(COUNT)):
                d = source_of(c, k, i)
                if k or i:
                    send(fo.at[k, h, i], rb.at[(NZ - d) % NZ], back_sem.at[0], dev(dz=d, core=h))
                elif h:
                    send(fo.at[0, 1, 0], rb.at[4 * c], back_sem.at[1 - c], dev(dz=d, core=1))
                else:
                    pl.when(c == 0)(back_self.start)
                    pl.when(c == 1)(back_near.start)

    back_self = pltpu.make_async_copy(fo.at[0, 0, 0], rb.at[0], back_sem.at[1])
    back_near = pltpu.make_async_remote_copy(
        src_ref=fo.at[0, 0, 0], dst_ref=rb.at[4], send_sem=self_send.at[1], recv_sem=back_sem.at[0],
        device_id=dev(dz=-4, core=0), device_id_type=MESH)

    gather_start(0)
    hand_on(0)
    gather_start(1)
    hand_on(1)
    for load in loads[3:]:
        load.wait()
    for copy in to_twin:
        copy.wait_recv()
    gather_end(0)
    spread(0, hidden_of(0))
    gather_end(1)
    spread(1, hidden_of(1))
    sum_first(0)
    sum_first(1)
    send_back(0)
    send_back(1)

    arrived(rb.at[0], back_sem.at[1])
    arrived(rb.at[pl.ds(1, NZ - 1)], back_sem.at[0])
    terms = jnp.dot(mix[...], rb[...].reshape(256, LANES), preferred_element_type=F32)
    mixed = terms[:64] + terms[64:128] + terms[128:]
    for j in range(PIECES):
        out_ref[:, j * LANES:(j + 1) * LANES] = mixed[j * 16:(j + 1) * 16].astype(BF16)

    for copy in sent + to_twin:
        copy.wait_send()
    pl.when(c == 1)(to_near.wait_send)
    pl.when(c == 1)(back_near.wait_send)


def on_device(tokens, expert_ids, route_weights, gate_weight, up_weight, down_weight):
    dma = lambda *shape: pltpu.SemaphoreType.DMA(shape)
    vmem = pltpu.VMEM
    return pl.pallas_call(
        kernel,
        out_shape=jax.ShapeDtypeStruct((16, 512), BF16),
        in_specs=[pl.BlockSpec(memory_space=pltpu.HBM)] * 6,
        out_specs=pl.BlockSpec(memory_space=pltpu.VMEM),
        scratch_shapes=[
            vmem((16, 512), BF16), vmem((3, 16), jnp.int32), vmem((3, 16), F32),
            vmem((2 * HID, 4096), BF16), vmem((2 * HID, 4096), BF16), vmem((8, 2 * HID, 512), BF16),
            vmem((16, 16, LANES), BF16), vmem((192, 256), BF16),
            vmem((4, 16, LANES), BF16), vmem((3, 16, LANES), BF16),
            vmem((2, 2, COUNT, 16, LANES), BF16),
            vmem((2, 2, 4, 4, ROWS, 512), BF16),
            vmem((2, 4, ROWS, 512), F32), vmem((2, 4, ROWS, 512), F32),
            vmem((2, 4, 3, ROWS, 512), BF16), vmem((2, 3, 4, ROWS, 512), BF16),
            vmem((2, 3, 4, ROWS, 512), BF16), vmem((2, 3, 4, ROWS, 512), BF16),
            vmem((2, 3, ROWS, 512), BF16), vmem((2, 3, ROWS, 512), BF16),
            vmem((2, 3, ROWS, 512), BF16), vmem((2, 3, ROWS, 512), BF16),
            vmem((2, 2, COUNT, 16, LANES), BF16), vmem((16, 16, LANES), BF16),
            dma(13), dma(10), dma(10), dma(160), dma(2), dma(2), dma(2), dma(2, 2, 3), dma(2, 2, 3),
            dma(2, 3), dma(2, 3), dma(2, 3), dma(2, 3), dma(2),
        ],
        compiler_params=pltpu.CompilerParams(
            collective_id=0, has_side_effects=True, vmem_limit_bytes=60 << 20),
        name="experts",
    )(tokens, expert_ids.T, route_weights.T, gate_weight, up_weight, down_weight)


def solution(mesh):
    placed = (
        P(("dp", "expert"), "tensor"),
        P(("dp", "expert"), None),
        P(("dp", "expert"), None),
        P("expert", ("dp", "tensor"), None),
        P("expert", ("dp", "tensor"), None),
        P("expert", ("dp", "tensor"), None),
    )
    return jax.shard_map(
        on_device,
        mesh=mesh,
        in_specs=placed,
        out_specs=P(("dp", "expert"), "tensor"),
        check_vma=False,
    )
```

```python
import jax
import jax.numpy as jnp
from jax import lax
from jax.experimental import pallas as pl
from jax.experimental.pallas import tpu as pltpu
from jax.sharding import PartitionSpec as P

MESH = pl.DeviceIdType.MESH
BF16 = jnp.bfloat16
F32 = jnp.float32
NZ = 16
SLOTS = 4
LANES = 128
PIECES = 4
HID = 160
UP = 384
COUNT = 4
ROWS = COUNT * SLOTS
FAR_FIRST = (2, 1, 3)
IN_ORDER = (0, 1, 3, 2)
LATER = (8, 9, 7, 10, 6, 11, 5)


def iota(shape, dim):
    return lax.broadcasted_iota(jnp.int32, shape, dim)


def source_of(core, k, i):
    return 4 * k + i - core * (4 + 8 * k)


def place_of(expert):
    source = (8 - expert) % NZ - 8
    if source >= 0:
        return 0, source // 4, source % 4
    return 1, int(source < -4), source % 4


def unfold_matrix(transposed):
    size = 16 * COUNT
    row, col = iota((size, size), 0), iota((size, size), 1)
    if transposed:
        row, col = col, row
    wanted = (row % ROWS) // SLOTS * 16 + row // ROWS * SLOTS + row % SLOTS
    return jnp.where(wanted == col, 1.0, 0.0).astype(BF16)


def kernel(tok_hbm, ids_hbm, rw_hbm, wg_hbm, wu_hbm, wd_hbm, out_ref,
           tok, ids, rw, wgu, wd, ob, mix, held, zr, xg, own0, own1, s1x, s1y, r1x, r1y, s2x, s2y, r2x, r2y, fo, rb,
           load_sem, twin_sem, twin_send, send_sem, self_send, z_sem, hold_sem, p1_sem, p2_sem, q1x_sem, q1y_sem, q2x_sem, q2y_sem,
           back_sem):
    x, z, t = lax.axis_index("dp"), lax.axis_index("expert"), lax.axis_index("tensor")
    y, c = t // 2, t % 2

    def dev(dx=0, dz=0, dy=0, core=c):
        return ((x + dx + 4) % 4, (z + dz + NZ) % NZ, (y + dy) % 4 * 2 + core)

    barrier = pltpu.get_barrier_semaphore()
    loads = [
        pltpu.make_async_copy(ids_hbm, ids, load_sem.at[0]),
        pltpu.make_async_copy(rw_hbm, rw, load_sem.at[1]),
        pltpu.make_async_copy(tok_hbm, tok, load_sem.at[2]),
        pltpu.make_async_copy(wg_hbm.at[0], wgu.at[pl.ds(0, HID)], load_sem.at[3]),
        pltpu.make_async_copy(wu_hbm.at[0], wgu.at[pl.ds(UP, HID)], load_sem.at[4]),
    ]
    for i in range(8):
        loads.append(pltpu.make_async_copy(wd_hbm.at[0, :, pl.ds(i * 512, 512)], wd.at[i, pl.ds(0, HID)], load_sem.at[5 + i]))
    for load in loads[:3]:
        load.start()
    partners = [dict(dz=d, core=core) for d in (4, -4, 3, -3, 2, -2, 1, -1) for core in range(2)]
    partners += [dict(dx=d) for d in FAR_FIRST] + [dict(dy=d) for d in FAR_FIRST] + [dict(core=1 - c)]
    for partner in partners:
        pl.semaphore_signal(barrier, inc=1, device_id=dev(**partner), device_id_type=MESH)
    for load in loads[3:]:
        load.start()

    sent = []

    def send(src, dst, sem, device):
        copy = pltpu.make_async_remote_copy(
            src_ref=src, dst_ref=dst, send_sem=send_sem.at[len(sent)], recv_sem=sem,
            device_id=device, device_id_type=MESH)
        copy.start()
        sent.append(copy)

    def arrived(ref, sem):
        pltpu.make_async_copy(ref, ref, sem).wait()

    for load in loads[:3]:
        load.wait()
    shape = (256, 64)
    q, lane = iota(shape, 0), iota(shape, 1)
    steps_up = (ids[...] - z + NZ) % NZ
    ids_wide = jnp.concatenate([steps_up] * PIECES, axis=1)
    rw_wide = jnp.concatenate([rw[...]] * PIECES, axis=1)
    hits = [ids_wide[k:k + 1] == q // 16 for k in range(3)]
    hit = jnp.where(hits[0] | hits[1] | hits[2], 1.0, 0.0)
    source, row = iota((64, 64), 0), iota((64, 64), 1)
    below = jnp.where((source // 16 == row // 16) & (source < row), 1.0, 0.0)
    place = jnp.dot(hit.astype(BF16), below.astype(BF16), preferred_element_type=F32)
    here = (place == (q % SLOTS).astype(F32)) & (q // SLOTS % PIECES == lane // 16)
    picked = jnp.where(here, hit, 0.0).astype(BF16)
    weights = jnp.zeros(shape, F32)
    for k in range(3):
        weights = weights + jnp.where(hits[k] & here, rw_wide[k:k + 1], 0.0)
    token_pieces = jnp.concatenate([tok[:, j * LANES:(j + 1) * LANES] for j in range(PIECES)], axis=0)
    slot_rows = jnp.dot(picked, token_pieces, preferred_element_type=F32)
    ob[...] = slot_rows.astype(BF16).reshape(16, 16, LANES)
    unfold = unfold_matrix(False)
    fold = unfold_matrix(True)

    pl.semaphore_wait(barrier, len(partners))

    send(ob.at[pl.ds(5, 4)], held.at[pl.ds(0, 4)], hold_sem.at[0], dev(dz=4))
    send(ob.at[pl.ds(9, 3)], held.at[pl.ds(4, 3)], hold_sem.at[1], dev(dz=-4))
    for d in (4, -4, 3, -3, 2, -2, 1, -1):
        core, k, i = place_of(d)
        send(ob.at[d % NZ], zr.at[k, c, i], z_sem.at[k], dev(dz=d, core=core))
    to_self = pltpu.make_async_copy(ob.at[0], zr.at[0, 0, 0], z_sem.at[0])
    to_near = pltpu.make_async_remote_copy(
        src_ref=ob.at[0], dst_ref=zr.at[0, 1, 0], send_sem=self_send.at[0], recv_sem=z_sem.at[0],
        device_id=dev(core=0), device_id_type=MESH)
    pl.when(c == 0)(to_self.start)
    pl.when(c == 1)(to_near.start)

    to_twin = []

    def twin(src, dst):
        n = len(to_twin)
        copy = pltpu.make_async_remote_copy(
            src_ref=src, dst_ref=dst, send_sem=twin_send.at[n], recv_sem=twin_sem.at[n],
            device_id=dev(core=1 - c), device_id_type=MESH)
        copy.start()
        to_twin.append(copy)

    twin(wg_hbm.at[0], wgu.at[pl.ds(HID, HID)])
    twin(wu_hbm.at[0], wgu.at[pl.ds(UP + HID, HID)])
    for i in range(8):
        twin(wd_hbm.at[0, :, pl.ds(i * 512, 512)], wd.at[i, pl.ds(HID, HID)])

    wgu[2 * HID:UP] = jnp.zeros((UP - 2 * HID, 4096), BF16)
    by_row = weights.T
    high = by_row.astype(BF16)
    rest = by_row - high.astype(F32)
    middle = rest.astype(BF16)
    mix[0:64] = high
    mix[64:128] = middle
    mix[128:192] = (rest - middle.astype(F32)).astype(BF16)

    arrived(held.at[pl.ds(0, 4)], hold_sem.at[0])
    arrived(held.at[pl.ds(4, 3)], hold_sem.at[1])
    for n in LATER:
        core, k, i = place_of(n)
        send(held.at[n - 5], zr.at[k, c, i], z_sem.at[k], dev(dz=n - 4 if n <= 8 else n - 12, core=core))

    def forward(k, h, i):
        if h == 0:
            place = xg.at[k, 0, y, (4 - i) % 4]
            if i:
                arrived(place, p1_sem.at[k, 0, i - 1])
            for j in FAR_FIRST:
                send(place, place, p2_sem.at[k, 0, j - 1], dev(dy=j))
        else:
            line = (y - i + 4) % 4
            place = xg.at[k, 1, line, 0]
            if i:
                arrived(place, p1_sem.at[k, 1, i - 1])
            for j in FAR_FIRST:
                send(place, xg.at[k, 1, line, 4 - j], p2_sem.at[k, 1, j - 1], dev(dx=j))

    def gather_start(k):
        arrived(zr.at[k], z_sem.at[k])
        for h in range(2):
            rows = jnp.dot(unfold, zr[k, h].reshape(COUNT * 16, LANES), preferred_element_type=F32).astype(BF16)
            for j in range(PIECES):
                xg[k, h, y, 0, :, j * LANES:(j + 1) * LANES] = rows[j * ROWS:(j + 1) * ROWS]
            for i in FAR_FIRST:
                if h == 0:
                    send(xg.at[k, 0, y, 0], xg.at[k, 0, y, 4 - i], p1_sem.at[k, 0, i - 1], dev(dx=i))
                else:
                    send(xg.at[k, 1, y, 0], xg.at[k, 1, y, 0], p1_sem.at[k, 1, i - 1], dev(dy=i))
        for h in range(2):
            forward(k, h, 0)

    def hand_on(k):
        for i in IN_ORDER[1:]:
            for h in range(2):
                forward(k, h, i)

    def project(k, h, line):
        left = xg[k, h, line].reshape(4 * ROWS, 512)
        right = wgu[:, pl.ds(pl.multiple_of((line * 2 + h) * 512, 512), 512)]
        return lax.dot_general(left, right, (((1,), (1,)), ((), ())), preferred_element_type=F32)

    def hidden_of(k):
        both = project(k, 0, y)
        for j in IN_ORDER[1:]:
            line = (y - j + 4) % 4
            arrived(xg.at[k, 0, line], p2_sem.at[k, 0, j - 1])
            both = both + project(k, 0, line)
        for j in IN_ORDER[1:]:
            arrived(xg.at[k, 1, pl.ds(0, 4), 4 - j], p2_sem.at[k, 1, j - 1])
        for line in range(4):
            both = both + project(k, 1, line)
        gate, up = both[:, :2 * HID], both[:, UP:]
        return (gate / (1.0 + jnp.exp(-gate)) * up).astype(BF16)

    def spread(k, hidden):
        for j in FAR_FIRST + (0,):
            for h in range(2):
                out = jnp.dot(hidden, wd[(y + j) % 4 * 2 + h], preferred_element_type=F32).reshape(4, ROWS, 512)
                if h == 0:
                    own0[k, j] = out[0]
                    s1x[k, j] = out[1:].astype(BF16)
                    for i in FAR_FIRST:
                        send(s1x.at[k, j, i - 1], r1x.at[k, i - 1, j], q1x_sem.at[k, i - 1], dev(dx=i))
                elif j:
                    s1y[k, j - 1] = out.astype(BF16)
                    send(s1y.at[k, j - 1], r1y.at[k, j - 1], q1y_sem.at[k, j - 1], dev(dy=j))
                else:
                    own1[k] = out

    def sum_first(k):
        for n in range(3):
            arrived(r1y.at[k, n], q1y_sem.at[k, n])
        for i in FAR_FIRST + (0,):
            total = own1[k, i]
            for n in range(3):
                total = total + r1y[k, n, i].astype(F32)
            if i:
                s2y[k, i - 1] = total.astype(BF16)
                send(s2y.at[k, i - 1], r2y.at[k, i - 1], q2y_sem.at[k, i - 1], dev(dx=i))
            else:
                own1[k, 0] = total
        for n in range(3):
            arrived(r1x.at[k, n], q1x_sem.at[k, n])
        for j in FAR_FIRST + (0,):
            total = own0[k, j]
            for n in range(3):
                total = total + r1x[k, n, j].astype(F32)
            if j:
                s2x[k, j - 1] = total.astype(BF16)
                send(s2x.at[k, j - 1], r2x.at[k, j - 1], q2x_sem.at[k, j - 1], dev(dy=j))
            else:
                own0[k, 0] = total

    def send_back(k):
        for h, own, landed, sem in ((1, own1, r2y, q2y_sem), (0, own0, r2x, q2x_sem)):
            total = own[k, 0]
            for n in range(3):
                arrived(landed.at[k, n], sem.at[k, n])
                total = total + landed[k, n].astype(F32)
            total = total.astype(BF16)
            pieces = [total[:, j * LANES:(j + 1) * LANES] for j in range(PIECES)]
            rows = jnp.dot(fold, jnp.concatenate(pieces, axis=0), preferred_element_type=F32).astype(BF16)
            fo[k, h] = rows.reshape(COUNT, 16, LANES)
            for i in reversed(range(COUNT)):
                d = source_of(c, k, i)
                if k or i:
                    send(fo.at[k, h, i], rb.at[(NZ - d) % NZ], back_sem.at[0], dev(dz=d, core=h))
                elif h:
                    send(fo.at[0, 1, 0], rb.at[4 * c], back_sem.at[1 - c], dev(dz=d, core=1))
                else:
                    pl.when(c == 0)(back_self.start)
                    pl.when(c == 1)(back_near.start)

    back_self = pltpu.make_async_copy(fo.at[0, 0, 0], rb.at[0], back_sem.at[1])
    back_near = pltpu.make_async_remote_copy(
        src_ref=fo.at[0, 0, 0], dst_ref=rb.at[4], send_sem=self_send.at[1], recv_sem=back_sem.at[0],
        device_id=dev(dz=-4, core=0), device_id_type=MESH)

    gather_start(0)
    hand_on(0)
    for load in loads[3:]:
        load.wait()
    for copy in to_twin:
        copy.wait_recv()
    gather_start(1)
    hand_on(1)
    spread(0, hidden_of(0))
    spread(1, hidden_of(1))
    sum_first(0)
    sum_first(1)
    send_back(0)
    send_back(1)

    for copy in sent + to_twin:
        copy.wait_send()
    pl.when(c == 1)(to_near.wait_send)
    pl.when(c == 1)(back_near.wait_send)
    arrived(rb.at[0], back_sem.at[1])
    arrived(rb.at[pl.ds(1, NZ - 1)], back_sem.at[0])
    terms = jnp.dot(mix[...], rb[...].reshape(256, LANES), preferred_element_type=F32)
    mixed = terms[:64] + terms[64:128] + terms[128:]
    for j in range(PIECES):
        out_ref[:, j * LANES:(j + 1) * LANES] = mixed[j * 16:(j + 1) * 16].astype(BF16)


def on_device(tokens, expert_ids, route_weights, gate_weight, up_weight, down_weight):
    operands = (tokens, expert_ids.T, route_weights.T, gate_weight, up_weight, down_weight)
    operands = [pltpu.with_memory_space_constraint(operand, pltpu.HBM) for operand in operands]
    dma = lambda *shape: pltpu.SemaphoreType.DMA(shape)
    vmem = pltpu.VMEM
    return pl.pallas_call(
        kernel,
        out_shape=pltpu.VMEM((16, 512), BF16),
        in_specs=[pl.BlockSpec(memory_space=pltpu.HBM)] * 6,
        out_specs=pl.BlockSpec(memory_space=pltpu.VMEM),
        scratch_shapes=[
            vmem((16, 512), BF16), vmem((3, 16), jnp.int32), vmem((3, 16), F32),
            vmem((UP + 2 * HID, 4096), BF16), vmem((8, 2 * HID, 512), BF16),
            vmem((16, 16, LANES), BF16), vmem((192, 256), BF16),
            vmem((7, 16, LANES), BF16),
            vmem((2, 2, COUNT, 16, LANES), BF16),
            vmem((2, 2, 4, 4, ROWS, 512), BF16),
            vmem((2, 4, ROWS, 512), F32), vmem((2, 4, ROWS, 512), F32),
            vmem((2, 4, 3, ROWS, 512), BF16), vmem((2, 3, 4, ROWS, 512), BF16),
            vmem((2, 3, 4, ROWS, 512), BF16), vmem((2, 3, 4, ROWS, 512), BF16),
            vmem((2, 3, ROWS, 512), BF16), vmem((2, 3, ROWS, 512), BF16),
            vmem((2, 3, ROWS, 512), BF16), vmem((2, 3, ROWS, 512), BF16),
            vmem((2, 2, COUNT, 16, LANES), BF16), vmem((16, 16, LANES), BF16),
            dma(13), dma(10), dma(10), dma(160), dma(2), dma(2), dma(7), dma(2, 2, 3), dma(2, 2, 3),
            dma(2, 3), dma(2, 3), dma(2, 3), dma(2, 3), dma(2),
        ],
        compiler_params=pltpu.CompilerParams(
            collective_id=0, has_side_effects=True, vmem_limit_bytes=40 << 20),
        name="experts",
    )(*operands)


def solution(mesh):
    placed = (
        P(("dp", "expert"), "tensor"),
        P(("dp", "expert"), None),
        P(("dp", "expert"), None),
        P("expert", ("dp", "tensor"), None),
        P("expert", ("dp", "tensor"), None),
        P("expert", ("dp", "tensor"), None),
    )
    return jax.shard_map(
        on_device,
        mesh=mesh,
        in_specs=placed,
        out_specs=P(("dp", "expert"), "tensor"),
        check_vma=False,
    )
```

```python
import jax
import jax.numpy as jnp
from jax import lax
from jax.experimental import pallas as pl
from jax.experimental.pallas import tpu as pltpu
from jax.sharding import PartitionSpec as P

MESH = pl.DeviceIdType.MESH
BF16 = jnp.bfloat16
F32 = jnp.float32
NZ = 16
SLOTS = 4
LANES = 128
PIECES = 4
HID = 160
UP = 384
COUNT = 4
ROWS = COUNT * SLOTS
FAR_FIRST = (2, 1, 3)
IN_ORDER = (0, 1, 3, 2)
LAST_OWN = (2, 1, 3, 0)
LATER = (8, 9, 7, 10, 6, 11, 5)


def iota(shape, dim):
    return lax.broadcasted_iota(jnp.int32, shape, dim)


def source_of(core, k, i):
    return 4 * k + i - core * (4 + 8 * k)


def place_of(expert):
    source = (8 - expert) % NZ - 8
    if source >= 0:
        return 0, source // 4, source % 4
    return 1, int(source < -4), source % 4


def unfold_matrix(transposed):
    size = 16 * COUNT
    row, col = iota((size, size), 0), iota((size, size), 1)
    if transposed:
        row, col = col, row
    wanted = (row % ROWS) // SLOTS * 16 + row // ROWS * SLOTS + row % SLOTS
    return jnp.where(wanted == col, 1.0, 0.0).astype(BF16)


def kernel(tok_hbm, ids_hbm, rw_hbm, wg_hbm, wu_hbm, wd_hbm, out_ref,
           tok, ids, rw, wgu, wd, ob, mix, held, zr, xg, own0, own1, s1x, s1y, r1x, r1y, s2x, s2y, r2x, r2y, fo, rb,
           load_sem, twin_sem, twin_send, send_sem, self_send, z_sem, hold_sem, p1_sem, p2_sem, q1x_sem, q1y_sem, q2x_sem, q2y_sem,
           back_sem):
    x, z, t = lax.axis_index("dp"), lax.axis_index("expert"), lax.axis_index("tensor")
    y, c = t // 2, t % 2

    def dev(dx=0, dz=0, dy=0, core=c):
        return ((x + dx + 4) % 4, (z + dz + NZ) % NZ, (y + dy) % 4 * 2 + core)

    barrier = pltpu.get_barrier_semaphore()
    loads = [
        pltpu.make_async_copy(ids_hbm, ids, load_sem.at[0]),
        pltpu.make_async_copy(rw_hbm, rw, load_sem.at[1]),
        pltpu.make_async_copy(tok_hbm, tok, load_sem.at[2]),
        pltpu.make_async_copy(wg_hbm.at[0], wgu.at[pl.ds(0, HID)], load_sem.at[3]),
        pltpu.make_async_copy(wu_hbm.at[0], wgu.at[pl.ds(UP, HID)], load_sem.at[4]),
    ]
    for i in range(8):
        loads.append(pltpu.make_async_copy(wd_hbm.at[0, :, pl.ds(i * 512, 512)], wd.at[i, pl.ds(0, HID)], load_sem.at[5 + i]))
    for load in loads[:3]:
        load.start()
    side = 1 - 2 * c
    partners = [dict(dz=side * d, core=core) for d in (4, 3, 2, 1) for core in range(2)] + [dict(dz=-4 * side)]
    partners += [dict(dx=d) for d in FAR_FIRST] + [dict(dy=d) for d in FAR_FIRST] + [dict(core=1 - c)]
    for partner in partners:
        pl.semaphore_signal(barrier, inc=1, device_id=dev(**partner), device_id_type=MESH)
    for load in loads[3:]:
        load.start()

    sent = []

    def send(src, dst, sem, device):
        copy = pltpu.make_async_remote_copy(
            src_ref=src, dst_ref=dst, send_sem=send_sem.at[len(sent)], recv_sem=sem,
            device_id=device, device_id_type=MESH)
        copy.start()
        sent.append(copy)

    def arrived(ref, sem):
        pltpu.make_async_copy(ref, ref, sem).wait()

    for load in loads[:3]:
        load.wait()
    shape = (256, 64)
    q, lane = iota(shape, 0), iota(shape, 1)
    steps_up = (ids[...] - z + NZ) % NZ
    ids_wide = jnp.concatenate([steps_up] * PIECES, axis=1)
    rw_wide = jnp.concatenate([rw[...]] * PIECES, axis=1)
    hits = [ids_wide[k:k + 1] == q // 16 for k in range(3)]
    hit = jnp.where(hits[0] | hits[1] | hits[2], 1.0, 0.0)
    source, row = iota((64, 64), 0), iota((64, 64), 1)
    below = jnp.where((source // 16 == row // 16) & (source < row), 1.0, 0.0)
    place = jnp.dot(hit.astype(BF16), below.astype(BF16), preferred_element_type=F32)
    here = (place == (q % SLOTS).astype(F32)) & (q // SLOTS % PIECES == lane // 16)
    picked = jnp.where(here, hit, 0.0).astype(BF16)
    weights = jnp.zeros(shape, F32)
    for k in range(3):
        weights = weights + jnp.where(hits[k] & here, rw_wide[k:k + 1], 0.0)
    token_pieces = jnp.concatenate([tok[:, j * LANES:(j + 1) * LANES] for j in range(PIECES)], axis=0)
    slot_rows = jnp.dot(picked, token_pieces, preferred_element_type=F32)
    ob[...] = slot_rows.astype(BF16).reshape(16, 16, LANES)
    unfold = unfold_matrix(False)
    fold = unfold_matrix(True)

    pl.semaphore_wait(barrier, len(partners))

    send(ob.at[pl.ds(5, 4)], held.at[pl.ds(0, 4)], hold_sem.at[0], dev(dz=4))
    send(ob.at[pl.ds(9, 3)], held.at[pl.ds(4, 3)], hold_sem.at[1], dev(dz=-4))
    for d in (4, -4, 3, -3, 2, -2, 1, -1):
        core, k, i = place_of(d)
        send(ob.at[d % NZ], zr.at[k, c, i], z_sem.at[k], dev(dz=d, core=core))
    to_self = pltpu.make_async_copy(ob.at[0], zr.at[0, 0, 0], z_sem.at[0])
    to_near = pltpu.make_async_remote_copy(
        src_ref=ob.at[0], dst_ref=zr.at[0, 1, 0], send_sem=self_send.at[0], recv_sem=z_sem.at[0],
        device_id=dev(core=0), device_id_type=MESH)
    pl.when(c == 0)(to_self.start)
    pl.when(c == 1)(to_near.start)

    to_twin = []

    def twin(src, dst):
        n = len(to_twin)
        copy = pltpu.make_async_remote_copy(
            src_ref=src, dst_ref=dst, send_sem=twin_send.at[n], recv_sem=twin_sem.at[n],
            device_id=dev(core=1 - c), device_id_type=MESH)
        copy.start()
        to_twin.append(copy)

    twin(wg_hbm.at[0], wgu.at[pl.ds(HID, HID)])
    twin(wu_hbm.at[0], wgu.at[pl.ds(UP + HID, HID)])
    for i in range(8):
        twin(wd_hbm.at[0, :, pl.ds(i * 512, 512)], wd.at[i, pl.ds(HID, HID)])

    wgu[2 * HID:UP] = jnp.zeros((UP - 2 * HID, 4096), BF16)
    by_row = weights.T
    high = by_row.astype(BF16)
    rest = by_row - high.astype(F32)
    middle = rest.astype(BF16)
    mix[0:64] = high
    mix[64:128] = middle
    mix[128:192] = (rest - middle.astype(F32)).astype(BF16)

    arrived(held.at[pl.ds(0, 4)], hold_sem.at[0])
    arrived(held.at[pl.ds(4, 3)], hold_sem.at[1])
    for n in LATER:
        core, k, i = place_of(n)
        send(held.at[n - 5], zr.at[k, c, i], z_sem.at[k], dev(dz=n - 4 if n <= 8 else n - 12, core=core))

    def forward(k, h, i):
        if h == 0:
            place = xg.at[k, 0, y, (4 - i) % 4]
            if i:
                arrived(place, p1_sem.at[k, 0, i - 1])
            for j in FAR_FIRST:
                send(place, place, p2_sem.at[k, 0, j - 1], dev(dy=j))
        else:
            line = (y - i + 4) % 4
            place = xg.at[k, 1, line, 0]
            if i:
                arrived(place, p1_sem.at[k, 1, i - 1])
            for j in FAR_FIRST:
                send(place, xg.at[k, 1, line, 4 - j], p2_sem.at[k, 1, j - 1], dev(dx=j))

    def gather_start(k):
        arrived(zr.at[k], z_sem.at[k])
        for h in range(2):
            rows = jnp.dot(unfold, zr[k, h].reshape(COUNT * 16, LANES), preferred_element_type=F32).astype(BF16)
            for j in range(PIECES):
                xg[k, h, y, 0, :, j * LANES:(j + 1) * LANES] = rows[j * ROWS:(j + 1) * ROWS]
            for i in FAR_FIRST:
                if h == 0:
                    send(xg.at[k, 0, y, 0], xg.at[k, 0, y, 4 - i], p1_sem.at[k, 0, i - 1], dev(dx=i))
                else:
                    send(xg.at[k, 1, y, 0], xg.at[k, 1, y, 0], p1_sem.at[k, 1, i - 1], dev(dy=i))
        for h in range(2):
            forward(k, h, 0)

    def hand_on(k):
        for i in IN_ORDER[1:]:
            for h in range(2):
                forward(k, h, i)

    def project(k, h, line):
        left = xg[k, h, line].reshape(4 * ROWS, 512)
        right = wgu[:, pl.ds(pl.multiple_of((line * 2 + h) * 512, 512), 512)]
        return lax.dot_general(left, right, (((1,), (1,)), ((), ())), preferred_element_type=F32)

    def hidden_of(k):
        both = project(k, 0, y)
        for j in IN_ORDER[1:]:
            line = (y - j + 4) % 4
            arrived(xg.at[k, 0, line], p2_sem.at[k, 0, j - 1])
            both = both + project(k, 0, line)
        for j in IN_ORDER[1:]:
            arrived(xg.at[k, 1, pl.ds(0, 4), 4 - j], p2_sem.at[k, 1, j - 1])
        for line in range(4):
            both = both + project(k, 1, line)
        gate, up = both[:, :2 * HID], both[:, UP:]
        return (gate / (1.0 + jnp.exp(-gate)) * up).astype(BF16)

    def spread(k, hidden):
        for j in LAST_OWN:
            out = jnp.dot(hidden, wd[(y + j) % 4 * 2], preferred_element_type=F32).reshape(4, ROWS, 512)
            own0[k, j] = out[0]
            s1x[k, j] = out[1:].astype(BF16)
            for i in FAR_FIRST:
                send(s1x.at[k, j, i - 1], r1x.at[k, i - 1, j], q1x_sem.at[k, i - 1, j], dev(dx=i))
            out = jnp.dot(hidden, wd[(y + j) % 4 * 2 + 1], preferred_element_type=F32).reshape(4, ROWS, 512)
            if j:
                s1y[k, j - 1] = out.astype(BF16)
            else:
                own1[k] = out
            if j == 3:
                for i in LAST_OWN:
                    for n in FAR_FIRST:
                        send(s1y.at[k, n - 1, i], r1y.at[k, n - 1, i], q1y_sem.at[k, n - 1, i], dev(dy=n))

    def sum_first(k):
        for i in LAST_OWN:
            for own, landed, sem, out, last, last_sem in (
                    (own1, r1y, q1y_sem, s2y, r2y, q2y_sem), (own0, r1x, q1x_sem, s2x, r2x, q2x_sem)):
                total = own[k, i]
                for n in FAR_FIRST:
                    arrived(landed.at[k, n - 1, i], sem.at[k, n - 1, i])
                    total = total + landed[k, n - 1, i].astype(F32)
                if i:
                    out[k, i - 1] = total.astype(BF16)
                    device = dev(dx=i) if own is own1 else dev(dy=i)
                    send(out.at[k, i - 1], last.at[k, i - 1], last_sem.at[k, i - 1], device)
                else:
                    own[k, 0] = total

    def send_back(k):
        for h, own, landed, sem in ((1, own1, r2y, q2y_sem), (0, own0, r2x, q2x_sem)):
            total = own[k, 0]
            for n in range(3):
                arrived(landed.at[k, n], sem.at[k, n])
                total = total + landed[k, n].astype(F32)
            total = total.astype(BF16)
            pieces = [total[:, j * LANES:(j + 1) * LANES] for j in range(PIECES)]
            rows = jnp.dot(fold, jnp.concatenate(pieces, axis=0), preferred_element_type=F32).astype(BF16)
            fo[k, h] = rows.reshape(COUNT, 16, LANES)
            for i in reversed(range(COUNT)):
                d = source_of(c, k, i)
                if k or i:
                    send(fo.at[k, h, i], rb.at[(NZ - d) % NZ], back_sem.at[0], dev(dz=d, core=h))
                elif h:
                    send(fo.at[0, 1, 0], rb.at[4 * c], back_sem.at[1 - c], dev(dz=d, core=1))
                else:
                    pl.when(c == 0)(back_self.start)
                    pl.when(c == 1)(back_near.start)

    back_self = pltpu.make_async_copy(fo.at[0, 0, 0], rb.at[0], back_sem.at[1])
    back_near = pltpu.make_async_remote_copy(
        src_ref=fo.at[0, 0, 0], dst_ref=rb.at[4], send_sem=self_send.at[1], recv_sem=back_sem.at[0],
        device_id=dev(dz=-4, core=0), device_id_type=MESH)

    gather_start(0)
    hand_on(0)
    for load in loads[3:]:
        load.wait()
    for copy in to_twin:
        copy.wait_recv()
    gather_start(1)
    hand_on(1)
    spread(0, hidden_of(0))
    spread(1, hidden_of(1))
    sum_first(0)
    sum_first(1)
    send_back(0)
    send_back(1)

    for copy in sent + to_twin:
        copy.wait_send()
    pl.when(c == 1)(to_near.wait_send)
    pl.when(c == 1)(back_near.wait_send)
    arrived(rb.at[0], back_sem.at[1])
    arrived(rb.at[pl.ds(1, NZ - 1)], back_sem.at[0])
    terms = jnp.dot(mix[...], rb[...].reshape(256, LANES), preferred_element_type=F32)
    mixed = terms[:64] + terms[64:128] + terms[128:]
    for j in range(PIECES):
        out_ref[:, j * LANES:(j + 1) * LANES] = mixed[j * 16:(j + 1) * 16].astype(BF16)


def on_device(tokens, expert_ids, route_weights, gate_weight, up_weight, down_weight):
    operands = (tokens, expert_ids.T, route_weights.T, gate_weight, up_weight, down_weight)
    operands = [pltpu.with_memory_space_constraint(operand, pltpu.HBM) for operand in operands]
    dma = lambda *shape: pltpu.SemaphoreType.DMA(shape)
    vmem = pltpu.VMEM
    return pl.pallas_call(
        kernel,
        out_shape=pltpu.VMEM((16, 512), BF16),
        in_specs=[pl.BlockSpec(memory_space=pltpu.HBM)] * 6,
        out_specs=pl.BlockSpec(memory_space=pltpu.VMEM),
        scratch_shapes=[
            vmem((16, 512), BF16), vmem((3, 16), jnp.int32), vmem((3, 16), F32),
            vmem((UP + 2 * HID, 4096), BF16), vmem((8, 2 * HID, 512), BF16),
            vmem((16, 16, LANES), BF16), vmem((192, 256), BF16),
            vmem((7, 16, LANES), BF16),
            vmem((2, 2, COUNT, 16, LANES), BF16),
            vmem((2, 2, 4, 4, ROWS, 512), BF16),
            vmem((2, 4, ROWS, 512), F32), vmem((2, 4, ROWS, 512), F32),
            vmem((2, 4, 3, ROWS, 512), BF16), vmem((2, 3, 4, ROWS, 512), BF16),
            vmem((2, 3, 4, ROWS, 512), BF16), vmem((2, 3, 4, ROWS, 512), BF16),
            vmem((2, 3, ROWS, 512), BF16), vmem((2, 3, ROWS, 512), BF16),
            vmem((2, 3, ROWS, 512), BF16), vmem((2, 3, ROWS, 512), BF16),
            vmem((2, 2, COUNT, 16, LANES), BF16), vmem((16, 16, LANES), BF16),
            dma(13), dma(10), dma(10), dma(160), dma(2), dma(2), dma(7), dma(2, 2, 3), dma(2, 2, 3),
            dma(2, 3, 4), dma(2, 3, 4), dma(2, 3), dma(2, 3), dma(2),
        ],
        compiler_params=pltpu.CompilerParams(
            collective_id=0, has_side_effects=True, vmem_limit_bytes=40 << 20),
        name="experts",
    )(*operands)


def solution(mesh):
    placed = (
        P(("dp", "expert"), "tensor"),
        P(("dp", "expert"), None),
        P(("dp", "expert"), None),
        P("expert", ("dp", "tensor"), None),
        P("expert", ("dp", "tensor"), None),
        P("expert", ("dp", "tensor"), None),
    )
    return jax.shard_map(
        on_device,
        mesh=mesh,
        in_specs=placed,
        out_specs=P(("dp", "expert"), "tensor"),
        check_vma=False,
    )
```
